512 devices in a mesh: slab: 64 (over y, z_hi, x), field: 8 (over z_lo, core).
Axes of the slice: x: 4, y: 8, z: 8 (z_hi: 2, z_lo: 4; z = z_hi * 4 + z_lo), core: 2. Of those that a mesh axis runs over, the one named last changes fastest.
Arguments:
- conform: float32 [3, 256, 1024, 128], P(None, 'field', 'slab'), may hold values from -6 to 6
- velocity: float32 [2, 1024, 128], P(None, 'slab'), may hold values from -0.9 to 2.1
- solid_mask: int32 [1024, 128], P('slab'), may hold values from 0 to 1, as said below
- upwind: int32 [2, 1024, 128], P(None, 'slab'), may hold values from 0 to 1
- relax_time: float32 [256], P('field'), may hold values from 0.5 to 5
- wiener: bfloat16 [6, 3, 256, 1024, 128], P(None, None, 'field', 'slab'), may hold values from -6 to 6
Outputs:
- fields_out: float32 [3, 256, 1024, 128], P(None, 'field', 'slab')
- velocity_out: float32 [2, 1024, 128], P(None, 'slab')
The draws below stay inside these ranges and needn't reach their ends.
Inputs may be any that keep to these rules, and one draw needn't show every extreme that they name: `solid_mask`: each aligned 32 by 32 tile of cells holds one disc of radius 3 to 9; at least 70 percent of cells are fluid. `upwind`: 1 takes the difference toward the lower neighbour, 0 toward the higher.
All inputs are finite; a program needn't handle non-finite values.
Results may differ from the reference program's by a relative error of at most 0.0003.
Values may be sent and summed in bfloat16 or wider, within the bound.
No kernel may reach another device: no remote copies, remote signals or barrier semaphores. Data moves between devices by JAX's collectives and lax.ppermute only.
A program may use at most 64 MiB of HBM per device.

```python
import math
import jax
import jax.numpy as jnp
from jax import lax

FIELDS = 256
NY = 128
STEPS = 2
SUBS = 3
NX = 1024


def draw_velocity(key, part):
    key = jax.random.fold_in(key, 7)
    first_key = jax.random.fold_in(key, 0)
    position = jnp.arange(NX, dtype=jnp.float32) / NX
    ramp = 0.4 + 0.8 * position
    rough = 0.3 * jnp.clip(jax.random.normal(first_key, (2, NX, NY), jnp.float32), -3.0, 3.0)
    along = ramp[:, None] + rough[0]
    return jnp.stack([along, rough[1]]).astype(jnp.float32)


def draw_solid_mask(key, part):
    key = jax.random.fold_in(key, 11)
    radius_key, row_key, column_key = jax.random.split(key, 3)
    tiles_x = NX // 32
    tiles_y = NY // 32
    radius = jax.random.randint(radius_key, (tiles_x, tiles_y), 3, 10, jnp.int32)
    centre_x = jax.random.randint(row_key, (tiles_x, tiles_y), 10, 23, jnp.int32)
    centre_y = jax.random.randint(column_key, (tiles_x, tiles_y), 10, 23, jnp.int32)

    def expand(table):
        return jnp.repeat(jnp.repeat(table, 32, axis=0), 32, axis=1)
    inner_x = (jnp.arange(NX, dtype=jnp.int32) % 32)[:, None]
    inner_y = (jnp.arange(NY, dtype=jnp.int32) % 32)[None, :]
    offset_x = inner_x - expand(centre_x)
    offset_y = inner_y - expand(centre_y)
    reach = expand(radius)
    return (offset_x * offset_x + offset_y * offset_y <= reach * reach).astype(jnp.int32)


def touch_ends(drawn, rng, least, high):
    extent = drawn.shape
    spot = [jax.random.randint(jax.random.fold_in(rng, axis), (), 0, extent[axis]) for axis in range(len(extent))]
    drawn = drawn.at[tuple(spot)].set(least)
    longest = extent.index(max(extent))
    spot[longest] = (spot[longest] + 1) % extent[longest]
    return drawn.at[tuple(spot)].set(high)


def level_of(key, shape, shards, smallest, largest):
    def one(dim, blocks):
        heights = jax.random.uniform(jax.random.fold_in(jax.random.fold_in(key, 6), dim), (blocks,), jnp.float32, smallest / len(shards), largest / len(shards))
        return jnp.repeat(jnp.exp(heights), shape[dim] // blocks).reshape((-1,) + (1,) * (len(shape) - dim - 1))

    factor_of = one(*shards[0])
    for cut in shards[1:]:
        factor_of = factor_of * one(*cut)
    return factor_of


def centred(key, dims, deviation, most, cuts=(), kind=jnp.bfloat16):
    values = deviation * jax.random.normal(key, dims, jnp.float32)
    if cuts:
        values = values * level_of(key, dims, cuts, -0.22, 0.18)
    return jnp.clip(values, -most, most).astype(kind)


def setup_inputs(seed: int = 0) -> dict:
    keys = jax.random.split(jax.random.key(seed), 7)
    return {
        "conform": centred(keys[0], (3, FIELDS, NX, NY), 1.0, 6.0, ((1, 8), (2, 64)), jnp.float32),
        "velocity": draw_velocity(jax.random.fold_in(keys[6], 71), 0),
        "solid_mask": draw_solid_mask(jax.random.fold_in(keys[6], 71), 0),
        "upwind": touch_ends(jax.random.randint(keys[3], (2, NX, NY), 0, 2), jax.random.fold_in(keys[3], 1), 0, 1).astype(jnp.int32),
        "relax_time": jnp.clip(jnp.exp(math.log(5.0) - 2.3025851 * jax.random.uniform(keys[4], (FIELDS,), jnp.float32) ** level_of(keys[4], (FIELDS,), ((0, 8),), -0.2, 0.2)), 0.5, 5.0),
        "wiener": centred(keys[5], (STEPS * SUBS, 3, FIELDS, NX, NY), 1.0, 6.0, ((2, 8), (3, 64))),
    }


sub_step = 0.1
macro_step = 0.3
viscosity = 0.5
modulus = 4.0
target_flow = 0.8

def gradients(speed):
    grad_x = (jnp.roll(speed, -1, 1) - jnp.roll(speed, 1, 1)) * 0.5
    grad_y = (jnp.roll(speed, -1, 2) - jnp.roll(speed, 1, 2)) * 0.5
    return (grad_x, grad_y)

def advance(fields, speed, grad_x, grad_y, flags, kicks, decay, spread):
    back_x = fields - jnp.roll(fields, 1, 2)
    ahead_x = jnp.roll(fields, -1, 2) - fields
    slope_x = jnp.where(flags[0] == 1, back_x, ahead_x)
    back_y = fields - jnp.roll(fields, 1, 3)
    ahead_y = jnp.roll(fields, -1, 3) - fields
    slope_y = jnp.where(flags[1] == 1, back_y, ahead_y)
    transport = speed[0] * slope_x + speed[1] * slope_y
    comp_x = fields[0]
    comp_y = fields[1]
    stretch = jnp.stack([grad_x[0] * comp_x + grad_y[0] * comp_y, grad_x[1] * comp_x + grad_y[1] * comp_y, jnp.zeros_like(comp_x)])
    return fields + sub_step * (stretch - transport - decay * fields) + spread * kicks

def partial_stress(fields):
    comp_x = fields[0]
    comp_y = fields[1]
    return jnp.stack([lax.optimization_barrier(jnp.sum(comp_x * comp_x, axis=0)), lax.optimization_barrier(jnp.sum(comp_x * comp_y, axis=0)), lax.optimization_barrier(jnp.sum(comp_y * comp_y, axis=0))])

def update(speed, stress, fluid, mean_flow):
    laplace = jnp.roll(speed, 1, 1) + jnp.roll(speed, -1, 1) + jnp.roll(speed, 1, 2) + jnp.roll(speed, -1, 2) - 4.0 * speed
    div_x = (jnp.roll(stress[0], -1, 0) - jnp.roll(stress[0], 1, 0)) * 0.5 + (jnp.roll(stress[1], -1, 1) - jnp.roll(stress[1], 1, 1)) * 0.5
    div_y = (jnp.roll(stress[1], -1, 0) - jnp.roll(stress[1], 1, 0)) * 0.5 + (jnp.roll(stress[2], -1, 1) - jnp.roll(stress[2], 1, 1)) * 0.5
    new_x = speed[0] + macro_step * (div_x + viscosity * laplace[0]) + (target_flow - mean_flow)
    new_y = speed[1] + macro_step * (div_y + viscosity * laplace[1])
    return fluid * jnp.stack([new_x, new_y])

def reference(conform, velocity, solid_mask, upwind, relax_time, wiener):
    fluid = (1 - solid_mask).astype(jnp.float32)
    block = math.gcd(FIELDS, 32)
    count = FIELDS // block
    fields = conform.reshape(3, count, block, NX, NY).transpose(1, 0, 2, 3, 4)
    relax = relax_time.reshape(count, block)
    speed = velocity
    for step_index in range(STEPS):
        grad_x, grad_y = gradients(speed)
        first = step_index * SUBS

        def one_block(total, items):
            block_fields, block_relax, which = items
            decay = (0.5 / block_relax)[:, None, None]
            spread = jnp.sqrt(sub_step / block_relax)[:, None, None]
            for sub_index in range(SUBS):
                kicks = lax.dynamic_slice_in_dim(wiener[first + sub_index], which * block, block, 1).astype(jnp.float32)
                block_fields = advance(block_fields, speed, grad_x, grad_y, upwind, kicks, decay, spread)
            return (total + partial_stress(block_fields), block_fields)
        summed, fields = lax.scan(one_block, jnp.zeros((3, NX, NY), jnp.float32), (fields, relax, jnp.arange(count, dtype=jnp.int32)))
        stress = modulus / FIELDS * summed - jnp.array([modulus, 0.0, modulus], jnp.float32)[:, None, None]
        mean_flow = jnp.sum(fluid * speed[0]) / jnp.sum(fluid)
        speed = update(speed, stress, fluid, mean_flow)
    fields_out = fields.transpose(1, 0, 2, 3, 4).reshape(3, FIELDS, NX, NY)
    return (fields_out, speed)
```

```python
import functools
import jax
import jax.numpy as jnp
from jax import lax
from jax.experimental import pallas as pl
from jax.experimental.pallas import tpu as pltpu
from jax.sharding import PartitionSpec as P

STEPS = 2
SUBS = 3
ROWS = 16
LANES = 128

sub_step = 0.1
macro_step = 0.3
viscosity = 0.5
modulus = 4.0
target_flow = 0.8

TRACKS = 3 * SUBS + 2
SENT = 3 * SUBS + 3 + 4
KEPT = 0.85
EXTRA = 16
TOP_ROW = ROWS + 3
BOTTOM_ROW = ROWS + 4
VMEM_LIMIT = 40 * 1024 * 1024


def left(v):
    return pltpu.roll(v, 1, 1)


def right(v):
    return pltpu.roll(v, LANES - 1, 1)


def above(v):
    return pltpu.roll(v, 1, 0)


def below(v):
    return pltpu.roll(v, v.shape[0] - 1, 0)


def row_index(rows):
    return lax.broadcasted_iota(jnp.int32, (rows, LANES), 0)


def neighbour_weights(speed, flag):
    step = sub_step * speed
    zero = jnp.zeros_like(step)
    return jnp.where(flag == 1, step, zero), jnp.where(flag == 1, zero, -step)


def split(v):
    first = v.astype(jnp.bfloat16).astype(jnp.float32)
    rest = v - first
    second = rest.astype(jnp.bfloat16).astype(jnp.float32)
    third = (rest - second).astype(jnp.bfloat16).astype(jnp.float32)
    return first, second, third


def updated_speed(fields_total, speed_ref, halo_ref, stress_ref, fluid):
    row = row_index(ROWS)
    scale = modulus / fields_total
    main = [scale * stress_ref[c, 0:ROWS, :] - (modulus if c != 1 else 0.0) for c in range(3)]
    before = [scale * stress_ref[c, TOP_ROW : TOP_ROW + 1, :] - (modulus if c != 1 else 0.0) for c in range(3)]
    after = [scale * stress_ref[c, BOTTOM_ROW : BOTTOM_ROW + 1, :] - (modulus if c != 1 else 0.0) for c in range(3)]
    mean_flow = stress_ref[0, ROWS : ROWS + 1, 0:1] / stress_ref[0, ROWS : ROWS + 1, 1:2]

    def up(v, edge):
        return jnp.where(row == 0, edge, above(v))

    def down(v, edge):
        return jnp.where(row == ROWS - 1, edge, below(v))

    new = []
    for c in range(2):
        v = speed_ref[c]
        laplace = up(v, halo_ref[c : c + 1, :]) + down(v, halo_ref[2 + c : 3 + c, :]) + left(v) + right(v) - 4.0 * v
        along_x = down(main[c], after[c]) - up(main[c], before[c])
        along_y = right(main[c + 1]) - left(main[c + 1])
        divergence = along_x * 0.5 + along_y * 0.5
        v = v + macro_step * (divergence + viscosity * laplace)
        if c == 0:
            v = v + (target_flow - mean_flow)
        new.append(fluid * v)
    return new


def own_kernel(nf, fields_total, first, *refs):
    refs = list(refs)
    delta_ref, spread_ref, odd_ref, speed_ref, solid_ref, upwind_ref, fields_ref, wiener_ref = refs[:8]
    rest = refs[8:]
    fluid = (1 - solid_ref[...]).astype(jnp.float32)
    if first:
        sx, sy = speed_ref[0], speed_ref[1]
    else:
        halo_ref, stress_ref = rest[:2]
        rest = rest[2:]
        sx, sy = updated_speed(fields_total, speed_ref, halo_ref, stress_ref, fluid)
    out_ref, top_ref, bottom_ref, send1_ref, send2_ref, sums_ref = rest[:6]
    rest = rest[6:]
    if not first:
        new_speed_ref = rest[0]
        rest = rest[1:]
        new_speed_ref[0] = sx
        new_speed_ref[1] = sy
    top_extra, bottom_extra = rest

    row = row_index(ROWS)
    zero = jnp.zeros((ROWS, LANES), jnp.float32)

    def grad_x(v):
        return (jnp.where(row == ROWS - 1, zero, below(v)) - jnp.where(row == 0, zero, above(v))) * 0.5

    def grad_y(v):
        return (right(v) - left(v)) * 0.5

    gxx, gxy = sub_step * grad_x(sx), sub_step * grad_x(sy)
    gyx, gyy = sub_step * grad_y(sx), sub_step * grad_y(sy)
    flag_x, flag_y = upwind_ref[0], upwind_ref[1]
    wa, wb = neighbour_weights(sx, flag_x)
    wl, wr = neighbour_weights(sy, flag_y)
    centre = 1.0 - wa - wb - wl - wr
    wa = jnp.where(row == 0, zero, wa)
    wb = jnp.where(row == ROWS - 1, zero, wb)

    def body(f, carry):
        base = centre - delta_ref[f]
        spread = spread_ref[f]
        diagonal = (base + gxx, base + gyy, base)
        q = [fields_ref[c, f] for c in range(3)]
        for k in range(SUBS):
            new = []
            for c in range(3):
                v = q[c]
                top_ref[3 * k + c, pl.ds(f, 1), :] = v[0:1, :]
                bottom_ref[3 * k + c, pl.ds(f, 1), :] = v[ROWS - 1 : ROWS, :]
                acc = diagonal[c] * v + spread * wiener_ref[k, c, f].astype(jnp.float32)
                acc = acc + (wl * left(v) + wr * right(v))
                acc = acc + (wa * above(v) + wb * below(v))
                if c == 0:
                    acc = acc + gyx * q[1]
                elif c == 1:
                    acc = acc + gxy * q[0]
                new.append(acc)
            q = new
        for c in range(3):
            out_ref[c, f] = q[c]
        for c in range(2):
            top_ref[3 * SUBS + c, pl.ds(f, 1), :] = q[c][0:1, :]
            bottom_ref[3 * SUBS + c, pl.ds(f, 1), :] = q[c][ROWS - 1 : ROWS, :]
        return carry

    lax.fori_loop(0, nf, body, 0, unroll=2)

    flow = jnp.sum(jnp.sum(fluid * sx, axis=0, keepdims=True), axis=1, keepdims=True)
    cells = jnp.sum(jnp.sum(fluid, axis=0, keepdims=True), axis=1, keepdims=True)
    lane = lax.broadcasted_iota(jnp.int32, (8, LANES), 1)
    flow = flow + jnp.zeros((8, LANES), jnp.float32)
    cells = cells + jnp.zeros((8, LANES), jnp.float32)
    sums_ref[...] = jnp.where(lane == 0, flow, jnp.where(lane == 1, cells, 0.0))
    packed = jnp.zeros((8, LANES), jnp.float32)
    for i, term in enumerate(split(flow) + split(cells)):
        packed = jnp.where(lane == i, term, packed)
    terms = (split(sx), split(sy))
    flags = (flag_x.astype(jnp.float32), flag_y.astype(jnp.float32))
    for extra, near, far in ((top_extra, 0, 1), (bottom_extra, ROWS - 1, ROWS - 2)):
        for c in range(2):
            for i in range(3):
                extra[3 * c + i : 3 * c + i + 1, :] = terms[c][i][near : near + 1, :]
                extra[6 + 3 * c + i : 7 + 3 * c + i, :] = terms[c][i][far : far + 1, :]
        extra[12:13, :] = flags[0][near : near + 1, :]
        extra[13:14, :] = flags[1][near : near + 1, :]
        extra[14:15, :] = flags[0][far : far + 1, :]
        extra[15:16, :] = packed[0:1, :]

    odd = jnp.full((nf, LANES), odd_ref[0], jnp.int32) == 1
    for send_ref, one_ref, other_ref in ((send1_ref, top_ref, bottom_ref), (send2_ref, bottom_ref, top_ref)):

        def put(t, v):
            rounded = v.astype(jnp.bfloat16)
            send_ref[nf * t : nf * t + nf, :] = rounded
            return v - rounded.astype(jnp.float32)

        for c in range(3):
            error = jnp.zeros((nf, LANES), jnp.float32)
            for k in range(SUBS):
                error = put(3 * k + c, jnp.where(odd, one_ref[3 * k + c], other_ref[3 * k + c]) + KEPT * error)
            put(3 * SUBS + c, error)
            if c < 2:
                error = put(3 * SUBS + 3 + c, jnp.where(odd, one_ref[3 * SUBS + c], other_ref[3 * SUBS + c]))
                put(3 * SUBS + 5 + c, error)
    odd = jnp.full((EXTRA, LANES), odd_ref[0], jnp.int32) == 1
    top, bottom = top_extra[...], bottom_extra[...]
    tail = nf * SENT
    send1_ref[tail : tail + EXTRA, :] = jnp.where(odd, top, bottom).astype(jnp.bfloat16)
    send2_ref[tail : tail + EXTRA, :] = jnp.where(odd, bottom, top).astype(jnp.bfloat16)


def join_kernel(nf, delta_ref, odd_ref, speed_ref, upwind_ref, own_ref, top_ref, bottom_ref, recv1_ref, recv2_ref,
                out_ref, stress_ref, halo_ref, before_ref, after_ref):
    tail = nf * SENT
    odd = jnp.full((nf, LANES), odd_ref[0], jnp.int32) == 1

    def track(ref, t):
        last = 3 * (SUBS - 1)
        if t < last:
            places = (t,)
        elif t < 3 * SUBS:
            places = (t, t + 3)
        else:
            places = (t + 3, t + 5)
        terms = [ref[nf * p : nf * p + nf, :].astype(jnp.float32) for p in places]
        return sum(terms[1:], terms[0])

    for t in range(TRACKS):
        one = track(recv1_ref, t)
        two = track(recv2_ref, t)
        before_ref[t] = jnp.where(odd, one, two)
        after_ref[t] = jnp.where(odd, two, one)
    odd = jnp.full((EXTRA, LANES), odd_ref[0], jnp.int32) == 1
    one = recv1_ref[tail : tail + EXTRA, :].astype(jnp.float32)
    two = recv2_ref[tail : tail + EXTRA, :].astype(jnp.float32)
    extras = (jnp.where(odd, one, two), jnp.where(odd, two, one))

    row = row_index(8)
    zero = jnp.zeros((8, LANES), jnp.float32)

    def joined(extra, i):
        return extra[i : i + 1, :] + extra[i + 1 : i + 2, :] + extra[i + 2 : i + 3, :]

    def strips(values, near, far):
        own_top = pltpu.roll(values[0:8], 4, 0)
        own_bottom = pltpu.roll(values[8:16], 4, 0)
        top = jnp.where(row >= 4, own_top, jnp.where(row == 3, near[0], jnp.where(row == 2, far[0], zero)))
        bottom = jnp.where(row < 4, own_bottom, jnp.where(row == 4, near[1], jnp.where(row == 5, far[1], zero)))
        return jnp.concatenate([top, bottom], axis=0)

    near_x = [joined(e, 0) for e in extras]
    near_y = [joined(e, 3) for e in extras]
    far_x = [joined(e, 6) for e in extras]
    far_y = [joined(e, 9) for e in extras]
    halo_ref[0:1, :] = near_x[0]
    halo_ref[1:2, :] = near_y[0]
    halo_ref[2:3, :] = near_x[1]
    halo_ref[3:4, :] = near_y[1]
    halo_ref[4:8, :] = jnp.zeros((4, LANES), jnp.float32)
    sx = strips(speed_ref[0], near_x, far_x)
    sy = strips(speed_ref[1], near_y, far_y)
    flag_x = strips(upwind_ref[0].astype(jnp.float32), [e[12:13, :] for e in extras], [e[14:15, :] for e in extras])
    flag_y = strips(upwind_ref[1].astype(jnp.float32), [e[13:14, :] for e in extras], [zero[0:1, :]] * 2)

    row2 = row_index(16)
    upper = (row2 == 3) | (row2 == 11)
    lower = (row2 == 4) | (row2 == 12)
    zero2 = jnp.zeros((16, LANES), jnp.float32)
    gxx = (0.5 * sub_step) * (below(sx) - above(sx))
    gxy = (0.5 * sub_step) * (below(sy) - above(sy))
    gyx = (0.5 * sub_step) * (right(sx) - left(sx))
    gyy = (0.5 * sub_step) * (right(sy) - left(sy))
    wa, wb = neighbour_weights(sx, flag_x)
    wl, wr = neighbour_weights(sy, flag_y)
    centre = 1.0 - wa - wb - wl - wr
    from_upper = jnp.where(lower, wa, zero2)
    from_lower = jnp.where(upper, wb, zero2)
    upper_x = jnp.where(upper, (0.5 * sub_step) * below(sx), zero2)
    upper_y = jnp.where(upper, (0.5 * sub_step) * below(sy), zero2)
    lower_x = jnp.where(lower, (-0.5 * sub_step) * above(sx), zero2)
    lower_y = jnp.where(lower, (-0.5 * sub_step) * above(sy), zero2)
    from_upper_x = from_upper + upper_x
    from_lower_x = from_lower + lower_x

    def spread_rows(first_ref, second_ref, t, f):
        return jnp.concatenate(
            [
                jnp.broadcast_to(first_ref[t, pl.ds(f, 1), :], (8, LANES)),
                jnp.broadcast_to(second_ref[t, pl.ds(f, 1), :], (8, LANES)),
            ],
            axis=0,
        )

    def body(f, sums):
        base = centre - delta_ref[f]
        diagonal = (base + gxx, base + gyy, base)
        d = None
        for k in range(SUBS):
            hu = [spread_rows(before_ref, bottom_ref, 3 * k + c, f) for c in range(3)]
            hl = [spread_rows(top_ref, after_ref, 3 * k + c, f) for c in range(3)]
            new = [
                from_upper_x * hu[0] + from_lower_x * hl[0],
                from_upper * hu[1] + from_lower * hl[1] + (upper_y * hu[0] + lower_y * hl[0]),
                from_upper * hu[2] + from_lower * hl[2],
            ]
            if d is not None:
                for c in range(3):
                    v = d[c]
                    acc = new[c] + diagonal[c] * v
                    acc = acc + (wl * left(v) + wr * right(v))
                    acc = acc + (wa * above(v) + wb * below(v))
                    if c == 0:
                        acc = acc + gyx * d[1]
                    elif c == 1:
                        acc = acc + gxy * d[0]
                    new[c] = acc
            d = new
        full = []
        edge = []
        for c in range(3):
            own = own_ref[c, f]
            top = own[0:8] + jnp.where(row < 4, pltpu.roll(d[c][0:8], 4, 0), zero)
            bottom = own[8:16] + jnp.where(row >= 4, pltpu.roll(d[c][8:16], 4, 0), zero)
            v = jnp.concatenate([top, bottom], axis=0)
            out_ref[c, f] = v
            if c < 2:
                t = 3 * SUBS + c
                full.append(v)
                edge.append(
                    jnp.where(
                        row < 4,
                        d[c][0:8] + jnp.broadcast_to(before_ref[t, pl.ds(f, 1), :], (8, LANES)),
                        d[c][8:16] + jnp.broadcast_to(after_ref[t, pl.ds(f, 1), :], (8, LANES)),
                    )
                )
        pairs = ((0, 0), (0, 1), (1, 1))
        return tuple(s + full[i] * full[j] for s, (i, j) in zip(sums[:3], pairs)) + tuple(
            s + edge[i] * edge[j] for s, (i, j) in zip(sums[3:], pairs)
        )

    sums = lax.fori_loop(0, nf, body, (zero2,) * 3 + (zero,) * 3, unroll=2)
    keep = (row == 3) | (row == 4)
    for c in range(3):
        stress_ref[c, 0:ROWS, :] = sums[c]
        stress_ref[c, ROWS : ROWS + 8, :] = jnp.where(keep, sums[3 + c], zero)


def last_kernel(fields_total, speed_ref, solid_ref, halo_ref, stress_ref, out_ref):
    fluid = (1 - solid_ref[...]).astype(jnp.float32)
    sx, sy = updated_speed(fields_total, speed_ref, halo_ref, stress_ref, fluid)
    out_ref[0] = sx
    out_ref[1] = sy


def vmem():
    return pl.BlockSpec(memory_space=pltpu.VMEM)


def smem():
    return pl.BlockSpec(memory_space=pltpu.SMEM)


def shaped(shape, dtype=jnp.float32):
    return jax.ShapeDtypeStruct(shape, dtype)


def whole(shape):
    return pl.BlockSpec(shape, lambda i: (0,) * len(shape))


def own_steps(step, fields_total, delta, spread, odd, speed, solid, upwind, fields, wiener, halo, stress):
    nf = fields.shape[1]
    first = step == 0
    size = nf * SENT + EXTRA
    extra = [] if first else [halo, stress]
    outs = [
        shaped(fields.shape),
        shaped((TRACKS, nf, LANES)),
        shaped((TRACKS, nf, LANES)),
        shaped((size, LANES), jnp.bfloat16),
        shaped((size, LANES), jnp.bfloat16),
        shaped((8, LANES)),
    ]
    if not first:
        outs.append(shaped(speed.shape))
    got = pl.pallas_call(
        functools.partial(own_kernel, nf, fields_total, first),
        grid=(1,),
        out_shape=outs,
        in_specs=[smem(), smem(), smem()]
        + [whole(v.shape) for v in (speed, solid, upwind, fields)]
        + [pl.BlockSpec((SUBS,) + wiener.shape[1:], lambda i: (step, 0, 0, 0, 0))]
        + [whole(v.shape) for v in extra],
        out_specs=[whole(o.shape) for o in outs],
        scratch_shapes=[pltpu.VMEM((EXTRA, LANES), jnp.float32)] * 2,
        compiler_params=pltpu.CompilerParams(vmem_limit_bytes=VMEM_LIMIT),
        name="own_steps",
    )(delta, spread, odd, speed, solid, upwind, fields, wiener, *extra)
    return got if not first else list(got) + [speed]


def join(delta, odd, speed, upwind, own, top, bottom, recv1, recv2):
    nf = own.shape[1]
    return pl.pallas_call(
        functools.partial(join_kernel, nf),
        out_shape=[shaped(own.shape), shaped((3, ROWS + 8, LANES)), shaped((8, LANES))],
        in_specs=[smem(), smem()] + [vmem()] * 7,
        out_specs=[vmem()] * 3,
        scratch_shapes=[pltpu.VMEM((TRACKS, nf, LANES), jnp.float32)] * 2,
        compiler_params=pltpu.CompilerParams(vmem_limit_bytes=VMEM_LIMIT),
        name="join",
    )(delta, odd, speed, upwind, own, top, bottom, recv1, recv2)


def last_speed(fields_total, speed, solid, halo, stress):
    return pl.pallas_call(
        functools.partial(last_kernel, fields_total),
        out_shape=shaped(speed.shape),
        in_specs=[vmem()] * 4,
        out_specs=vmem(),
        name="last_speed",
    )(speed, solid, halo, stress)


def swapped(value, axis, bit):
    count = lax.axis_size(axis)
    return lax.ppermute(value, axis, [(i, i ^ bit) for i in range(count)])


def flow_sums(sums, recv1, recv2):
    terms = recv1[recv1.shape[0] - 1, 0:6].astype(jnp.float32)
    value = sums[0, 0:2] + jnp.stack([terms[0] + terms[1] + terms[2], terms[3] + terms[4] + terms[5]])
    value = value + swapped(value, "slab", 2)
    value = value + swapped(value, "slab", 4)
    value, recv2 = lax.optimization_barrier((value, recv2))
    slabs, parts = lax.axis_size("slab"), lax.axis_size("field")
    assert slabs == 8 * parts
    pairs = [(((s + 8 * f) % slabs) * parts + f, s * parts + f) for s in range(slabs) for f in range(parts)]
    return lax.ppermute(value, ("slab", "field"), pairs), recv2


def field_sum(value):
    bit = 1
    while bit < lax.axis_size("field"):
        value = value + swapped(value, "field", bit)
        bit *= 2
    return value


def per_device(conform, velocity, solid_mask, upwind, relax_time, wiener):
    slabs = lax.axis_size("slab")
    fields_total = conform.shape[1] * lax.axis_size("field")
    odd = (lax.axis_index("slab") % 2).astype(jnp.int32).reshape(1)
    delta = sub_step * (0.5 / relax_time)
    spread = jnp.sqrt(sub_step / relax_time)
    near_pairs = [(i, i ^ 1) for i in range(slabs)]
    far_pairs = [(i, (i + 1) % slabs if i % 2 else (i - 1) % slabs) for i in range(slabs)]
    fields, speed, halo, stress = conform, velocity, None, None
    for step in range(STEPS):
        own, top, bottom, send1, send2, sums, speed = own_steps(
            step, fields_total, delta, spread, odd, speed, solid_mask, upwind, fields, wiener, halo, stress
        )
        recv1 = lax.ppermute(send1, "slab", near_pairs)
        recv2 = lax.ppermute(send2, "slab", far_pairs)
        flow, recv2 = flow_sums(sums, recv1, recv2)
        fields, stress, halo = join(delta, odd, speed, upwind, own, top, bottom, recv1, recv2)
        stress = stress.at[0, ROWS, 0:2].set(flow)
        stress = field_sum(stress)
    speed = last_speed(fields_total, speed, solid_mask, halo, stress)
    return (fields, speed)


def solution(mesh):
    placed = (
        P(None, "field", "slab", None),
        P(None, "slab", None),
        P("slab", None),
        P(None, "slab", None),
        P("field"),
        P(None, None, "field", "slab", None),
    )
    return jax.shard_map(
        per_device,
        mesh=mesh,
        in_specs=placed,
        out_specs=(P(None, "field", "slab", None), P(None, "slab", None)),
        check_vma=False,
    )
```

```python
import functools
import jax
import jax.numpy as jnp
from jax import lax
from jax.experimental import pallas as pl
from jax.experimental.pallas import tpu as pltpu
from jax.sharding import PartitionSpec as P

STEPS = 2
SUBS = 3
ROWS = 16
LANES = 128

sub_step = 0.1
macro_step = 0.3
viscosity = 0.5
modulus = 4.0
target_flow = 0.8

TRACKS = 3 * SUBS + 2
SENT = 3 * SUBS + 3 + 4
KEPT = 0.85
EXTRA = 16
TOP_ROW = ROWS + 3
BOTTOM_ROW = ROWS + 4
UNROLL = 4
VMEM_LIMIT = 32 * 1024 * 1024


def left(v):
    return pltpu.roll(v, 1, 1)


def right(v):
    return pltpu.roll(v, LANES - 1, 1)


def above(v):
    return pltpu.roll(v, 1, 0)


def below(v):
    return pltpu.roll(v, v.shape[0] - 1, 0)


def row_index(rows):
    return lax.broadcasted_iota(jnp.int32, (rows, LANES), 0)


def neighbour_weights(speed, flag):
    step = sub_step * speed
    zero = jnp.zeros_like(step)
    return jnp.where(flag == 1, step, zero), jnp.where(flag == 1, zero, -step)


def split(v):
    first = v.astype(jnp.bfloat16).astype(jnp.float32)
    rest = v - first
    second = rest.astype(jnp.bfloat16).astype(jnp.float32)
    third = (rest - second).astype(jnp.bfloat16).astype(jnp.float32)
    return first, second, third


def total(flow_ref, which):
    flow = jnp.sum(flow_ref[...], axis=0, keepdims=True)
    return flow[:, which : which + 1] + flow[:, which + 2 : which + 3] + flow[:, which + 4 : which + 5]


def updated_speed(fields_total, speed, halo_ref, stress_refs, flow_ref, fluid):
    row = row_index(ROWS)
    scale = modulus / fields_total

    def stress(c, rows):
        return scale * (stress_refs[0][c, rows, :] + stress_refs[1][c, rows, :]) - (modulus if c != 1 else 0.0)

    main = [stress(c, slice(0, ROWS)) for c in range(3)]
    before = [stress(c, slice(TOP_ROW, TOP_ROW + 1)) for c in range(3)]
    after = [stress(c, slice(BOTTOM_ROW, BOTTOM_ROW + 1)) for c in range(3)]
    mean_flow = total(flow_ref, 0) / total(flow_ref, 1)

    def up(v, edge):
        return jnp.where(row == 0, edge, above(v))

    def down(v, edge):
        return jnp.where(row == ROWS - 1, edge, below(v))

    new = []
    for c in range(2):
        v = speed[c]
        laplace = up(v, halo_ref[c : c + 1, :]) + down(v, halo_ref[2 + c : 3 + c, :]) + left(v) + right(v) - 4.0 * v
        along_x = down(main[c], after[c]) - up(main[c], before[c])
        along_y = right(main[c + 1]) - left(main[c + 1])
        divergence = along_x * 0.5 + along_y * 0.5
        v = v + macro_step * (divergence + viscosity * laplace)
        if c == 0:
            v = v + (target_flow - mean_flow)
        new.append(fluid * v)
    return new


def relaxation(relax_ref, f):
    relax = jnp.full((8, LANES), relax_ref[f], jnp.float32)
    return sub_step * (0.5 / relax), jnp.sqrt(sub_step / relax)


def doubled(v):
    return jnp.concatenate([v, v], axis=0)


def slab_weights(sx, sy, flag_x, flag_y):
    row = row_index(ROWS)
    zero = jnp.zeros((ROWS, LANES), jnp.float32)

    def grad_x(v):
        return (jnp.where(row == ROWS - 1, zero, below(v)) - jnp.where(row == 0, zero, above(v))) * 0.5

    def grad_y(v):
        return (right(v) - left(v)) * 0.5

    gxx, gxy = sub_step * grad_x(sx), sub_step * grad_x(sy)
    gyx, gyy = sub_step * grad_y(sx), sub_step * grad_y(sy)
    wa, wb = neighbour_weights(sx, flag_x)
    wl, wr = neighbour_weights(sy, flag_y)
    centre = 1.0 - wa - wb - wl - wr
    wa = jnp.where(row == 0, zero, wa)
    wb = jnp.where(row == ROWS - 1, zero, wb)
    return centre, wa, wb, wl, wr, gxx, gxy, gyx, gyy


def substep(q, diagonal, weights, extra):
    _, wa, wb, wl, wr, _, gxy, gyx, _ = weights
    new = []
    for c in range(3):
        v = q[c]
        acc = diagonal[c] * v + extra[c]
        acc = acc + (wl * left(v) + wr * right(v))
        acc = acc + (wa * above(v) + wb * below(v))
        if c == 0:
            acc = acc + gyx * q[1]
        elif c == 1:
            acc = acc + gxy * q[0]
        new.append(acc)
    return new


def edge_kernel(nf, fields_total, first, *refs):
    refs = list(refs)

    def take(count):
        taken = refs[:count]
        del refs[:count]
        return taken

    relax_ref, odd_ref, speed_ref, solid_ref, upwind_ref, fields_ref, wiener_ref = take(7)
    if not first:
        halo_ref, stress_ref, other_ref, flow_ref = take(4)
    top_ref, bottom_ref, send1_ref, send2_ref, sums_ref = take(5)
    if not first:
        (new_speed_ref,) = take(1)
    top_extra, bottom_extra = refs

    fluid = (1 - solid_ref[...]).astype(jnp.float32)
    sx, sy = speed_ref[0], speed_ref[1]
    if not first:
        sx, sy = updated_speed(fields_total, (sx, sy), halo_ref, (stress_ref, other_ref), flow_ref, fluid)
        new_speed_ref[0] = sx
        new_speed_ref[1] = sy
    flow = jnp.sum(jnp.sum(fluid * sx, axis=0, keepdims=True), axis=1, keepdims=True)
    cells = jnp.sum(jnp.sum(fluid, axis=0, keepdims=True), axis=1, keepdims=True)
    lane = lax.broadcasted_iota(jnp.int32, (1, LANES), 1)
    sums = jnp.where(lane == 0, flow, jnp.where(lane == 1, cells, 0.0))
    sums_ref[...] = sums

    row = row_index(8)
    flag_x, flag_y = upwind_ref[0], upwind_ref[1]

    def packed(v):
        return jnp.where(row < 4, v[0:8], v[8:16])

    weights = [packed(w) for w in slab_weights(sx, sy, flag_x, flag_y)]
    centre, gxx, gyy = weights[0], weights[5], weights[8]

    def body(f):
        delta, spread = relaxation(relax_ref, f)
        base = centre - delta
        diagonal = (base + gxx, base + gyy, base)
        q = [packed(fields_ref[c, f]) for c in range(3)]
        for k in range(SUBS + 1):
            for c in range(3 if k < SUBS else 2):
                top_ref[3 * k + c, pl.ds(f, 1), :] = q[c][0:1, :]
                bottom_ref[3 * k + c, pl.ds(f, 1), :] = q[c][7:8, :]
            if k < SUBS:
                kicks = [spread * packed(wiener_ref[k, c, f].astype(jnp.float32)) for c in range(3)]
                q = substep(q, diagonal, weights, kicks)

    def some(j, carry):
        for u in range(UNROLL):
            body(j * UNROLL + u)
        return carry

    lax.fori_loop(0, nf // UNROLL, some, 0)

    first_term, second_term, third_term = split(jnp.broadcast_to(sums, (8, LANES)))
    packed_sums = (first_term + pltpu.roll(second_term, 2, 1) + pltpu.roll(third_term, 4, 1))[0:1]
    terms = (split(sx), split(sy))
    flags = (flag_x.astype(jnp.float32), flag_y.astype(jnp.float32))
    for extra, near, far in ((top_extra, 0, 1), (bottom_extra, ROWS - 1, ROWS - 2)):
        for c in range(2):
            for i in range(3):
                extra[3 * c + i : 3 * c + i + 1, :] = terms[c][i][near : near + 1, :]
                extra[6 + 3 * c + i : 7 + 3 * c + i, :] = terms[c][i][far : far + 1, :]
        extra[12:13, :] = flags[0][near : near + 1, :]
        extra[13:14, :] = flags[1][near : near + 1, :]
        extra[14:15, :] = flags[0][far : far + 1, :]
        extra[15:16, :] = packed_sums

    odd = jnp.full((nf, LANES), odd_ref[0], jnp.int32) == 1
    for send_ref, one_ref, two_ref in ((send1_ref, top_ref, bottom_ref), (send2_ref, bottom_ref, top_ref)):

        def put(t, v):
            rounded = v.astype(jnp.bfloat16)
            send_ref[nf * t : nf * t + nf, :] = rounded
            return v - rounded.astype(jnp.float32)

        for c in range(3):
            error = jnp.zeros((nf, LANES), jnp.float32)
            for k in range(SUBS):
                error = put(3 * k + c, jnp.where(odd, one_ref[3 * k + c], two_ref[3 * k + c]) + KEPT * error)
            put(3 * SUBS + c, error)
            if c < 2:
                error = put(3 * SUBS + 3 + c, jnp.where(odd, one_ref[3 * SUBS + c], two_ref[3 * SUBS + c]))
                put(3 * SUBS + 5 + c, error)
    odd = jnp.full((EXTRA, LANES), odd_ref[0], jnp.int32) == 1
    top, bottom = top_extra[...], bottom_extra[...]
    tail = nf * SENT
    send1_ref[tail : tail + EXTRA, :] = jnp.where(odd, top, bottom).astype(jnp.bfloat16)
    send2_ref[tail : tail + EXTRA, :] = jnp.where(odd, bottom, top).astype(jnp.bfloat16)


def own_kernel(nf, relax_ref, speed_ref, upwind_ref, fields_ref, wiener_ref, out_ref):
    weights = slab_weights(speed_ref[0], speed_ref[1], upwind_ref[0], upwind_ref[1])
    centre, gxx, gyy = weights[0], weights[5], weights[8]

    def body(f):
        delta, spread = [doubled(v) for v in relaxation(relax_ref, f)]
        base = centre - delta
        diagonal = (base + gxx, base + gyy, base)
        q = [fields_ref[c, f] for c in range(3)]
        for k in range(SUBS):
            kicks = [spread * wiener_ref[k, c, f].astype(jnp.float32) for c in range(3)]
            q = substep(q, diagonal, weights, kicks)
        for c in range(3):
            out_ref[c, f] = q[c]

    def some(j, carry):
        for u in range(UNROLL):
            body(j * UNROLL + u)
        return carry

    lax.fori_loop(0, nf // UNROLL, some, 0)


def join_kernel(nf, first, *refs):
    refs = list(refs)
    relax_ref, side_ref, speed_ref, upwind_ref, own_ref, top_ref, bottom_ref, recv_ref = refs[:8]
    refs = refs[8:]
    if not first:
        stress_in, halo_in = refs[:2]
        refs = refs[2:]
    out_ref, stress_ref, halo_ref, upper_ref, lower_ref = refs
    side = side_ref[0]
    top = jnp.full((nf, LANES), side, jnp.int32) == 1
    last = 3 * (SUBS - 1)
    for t in range(TRACKS):
        if t < last:
            places = (t,)
        elif t < 3 * SUBS:
            places = (t, t + 3)
        else:
            places = (t + 3, t + 5)
        terms = [recv_ref[nf * p : nf * p + nf, :].astype(jnp.float32) for p in places]
        got = sum(terms[1:], terms[0])
        upper_ref[t] = jnp.where(top, got, bottom_ref[t])
        lower_ref[t] = jnp.where(top, top_ref[t], got)
    tail = nf * SENT
    extra = recv_ref[tail : tail + EXTRA, :].astype(jnp.float32)

    row = row_index(8)
    top = jnp.full((8, LANES), side, jnp.int32) == 1
    zero = jnp.zeros((8, LANES), jnp.float32)
    own_rows = (top & (row >= 4)) | (~top & (row < 4))
    near_row = (top & (row == 3)) | (~top & (row == 4))
    far_row = (top & (row == 2)) | (~top & (row == 5))

    def strip(values, near, far):
        own = pltpu.roll(jnp.where(top, values[0:8], values[8:16]), 4, 0)
        return jnp.where(own_rows, own, jnp.where(near_row, near, jnp.where(far_row, far, zero)))

    def joined(i):
        return extra[i : i + 1, :] + extra[i + 1 : i + 2, :] + extra[i + 2 : i + 3, :]

    near_x, near_y = joined(0), joined(3)
    halo = jnp.where(row % 2 == 0, near_x, near_y)
    mine = (top & (row < 2)) | (~top & (row >= 2) & (row < 4))
    halo = jnp.where(mine, halo, zero)
    halo_ref[...] = halo if first else halo + halo_in[...]
    sx = strip(speed_ref[0], near_x, joined(6))
    sy = strip(speed_ref[1], near_y, joined(9))
    flag_x = strip(upwind_ref[0].astype(jnp.float32), extra[12:13, :], extra[14:15, :])
    flag_y = strip(upwind_ref[1].astype(jnp.float32), extra[13:14, :], zero)

    upper = row == 3
    lower = row == 4
    half = 0.5 * sub_step
    gxx = half * (below(sx) - above(sx))
    gxy = half * (below(sy) - above(sy))
    gyx = half * (right(sx) - left(sx))
    gyy = half * (right(sy) - left(sy))
    wa, wb = neighbour_weights(sx, flag_x)
    wl, wr = neighbour_weights(sy, flag_y)
    centre = 1.0 - wa - wb - wl - wr
    weights = (centre, wa, wb, wl, wr, gxx, gxy, gyx, gyy)
    from_upper = jnp.where(lower, wa, zero)
    from_lower = jnp.where(upper, wb, zero)
    upper_y = jnp.where(upper, half * below(sy), zero)
    lower_y = jnp.where(lower, -half * above(sy), zero)
    from_upper_x = from_upper + jnp.where(upper, half * below(sx), zero)
    from_lower_x = from_lower + jnp.where(lower, -half * above(sx), zero)
    start = pl.multiple_of((1 - side) * 8, 8)

    def body(f, sums):
        delta, _ = relaxation(relax_ref, f)
        base = centre - delta
        diagonal = (base + gxx, base + gyy, base)

        def spread_row(ref, t):
            return jnp.broadcast_to(ref[t, pl.ds(f, 1), :], (8, LANES))

        d = None
        for k in range(SUBS):
            hu = [spread_row(upper_ref, 3 * k + c) for c in range(3)]
            hl = [spread_row(lower_ref, 3 * k + c) for c in range(3)]
            new = [
                from_upper_x * hu[0] + from_lower_x * hl[0],
                from_upper * hu[1] + from_lower * hl[1] + (upper_y * hu[0] + lower_y * hl[0]),
                from_upper * hu[2] + from_lower * hl[2],
            ]
            d = new if d is None else substep(d, diagonal, weights, new)
        full = []
        edge = []
        for c in range(3):
            half_rows = own_ref[c, f, pl.ds(start, 8), :]
            v = half_rows + pltpu.roll(jnp.where(own_rows, d[c], zero), 4, 0)
            out_ref[c, f, pl.ds(start, 8), :] = v
            rest = pl.multiple_of(8 - start, 8)
            out_ref[c, f, pl.ds(rest, 8), :] = own_ref[c, f, pl.ds(rest, 8), :]
            if c < 2:
                t = 3 * SUBS + c
                full.append(v)
                edge.append(d[c] + jnp.where(upper, spread_row(upper_ref, t), spread_row(lower_ref, t)))
        pairs = ((0, 0), (0, 1), (1, 1))
        return tuple(s + full[i] * full[j] for s, (i, j) in zip(sums[:3], pairs)) + tuple(
            s + edge[i] * edge[j] for s, (i, j) in zip(sums[3:], pairs)
        )

    def some(j, sums):
        for u in range(UNROLL):
            sums = body(j * UNROLL + u, sums)
        return sums

    sums = lax.fori_loop(0, nf // UNROLL, some, (zero,) * 6)
    for c in range(3):
        edge = jnp.where(near_row, sums[3 + c], zero)
        if first:
            stress_ref[c, 0:ROWS, :] = jnp.zeros((ROWS, LANES), jnp.float32)
        else:
            stress_ref[c, 0:ROWS, :] = stress_in[c, 0:ROWS, :]
            edge = edge + stress_in[c, ROWS : ROWS + 8, :]
        stress_ref[c, pl.ds(start, 8), :] = sums[c]
        stress_ref[c, ROWS : ROWS + 8, :] = edge


def last_kernel(fields_total, speed_ref, solid_ref, halo_ref, stress_ref, other_ref, flow_ref, out_ref):
    fluid = (1 - solid_ref[...]).astype(jnp.float32)
    speed = (speed_ref[0], speed_ref[1])
    sx, sy = updated_speed(fields_total, speed, halo_ref, (stress_ref, other_ref), flow_ref, fluid)
    out_ref[0] = sx
    out_ref[1] = sy


def vmem():
    return pl.BlockSpec(memory_space=pltpu.VMEM)


def smem():
    return pl.BlockSpec(memory_space=pltpu.SMEM)


def shaped(shape, dtype=jnp.float32):
    return jax.ShapeDtypeStruct(shape, dtype)


def whole(shape):
    return pl.BlockSpec(shape, lambda i: (0,) * len(shape))


def step_block(step, shape):
    return pl.BlockSpec((SUBS,) + shape[1:], lambda i: (step,) + (0,) * (len(shape) - 1))


def cost(flops, *arrays):
    size = sum(v.size * v.dtype.itemsize for v in arrays)
    return pl.CostEstimate(flops=flops, bytes_accessed=size, transcendentals=0)


def params():
    return pltpu.CompilerParams(vmem_limit_bytes=VMEM_LIMIT)


def edge_steps(step, fields_total, relax, odd, speed, solid, upwind, fields, wiener, extra):
    nf = fields.shape[1]
    first = step == 0
    size = nf * SENT + EXTRA
    outs = [
        shaped((TRACKS, nf, LANES)),
        shaped((TRACKS, nf, LANES)),
        shaped((size, LANES), jnp.bfloat16),
        shaped((size, LANES), jnp.bfloat16),
        shaped((1, LANES)),
    ]
    if not first:
        outs.append(shaped(speed.shape))
    got = pl.pallas_call(
        functools.partial(edge_kernel, nf, fields_total, first),
        grid=(1,),
        out_shape=outs,
        in_specs=[smem(), smem()]
        + [whole(v.shape) for v in (speed, solid, upwind, fields)]
        + [step_block(step, wiener.shape)]
        + [whole(v.shape) for v in extra],
        out_specs=[whole(o.shape) for o in outs],
        scratch_shapes=[pltpu.VMEM((EXTRA, LANES), jnp.float32)] * 2,
        compiler_params=params(),
        name="edge_steps",
    )(relax, odd, speed, solid, upwind, fields, wiener, *extra)
    return list(got) + ([speed] if first else [])


def own_steps(step, relax, speed, upwind, fields, wiener):
    return pl.pallas_call(
        functools.partial(own_kernel, fields.shape[1]),
        grid=(1,),
        out_shape=shaped(fields.shape),
        in_specs=[smem()] + [whole(v.shape) for v in (speed, upwind, fields)] + [step_block(step, wiener.shape)],
        out_specs=whole(fields.shape),
        compiler_params=params(),
        cost_estimate=cost(60 * fields.size, fields, fields, fields),
        name="own_steps",
    )(relax, speed, upwind, fields, wiener)


def join(relax, side, speed, upwind, own, top, bottom, recv, before=()):
    nf = own.shape[1]
    return pl.pallas_call(
        functools.partial(join_kernel, nf, not before),
        out_shape=[shaped(own.shape), shaped((3, ROWS + 8, LANES)), shaped((8, LANES))],
        in_specs=[smem(), smem()] + [vmem()] * (6 + len(before)),
        out_specs=[vmem()] * 3,
        scratch_shapes=[pltpu.VMEM((TRACKS, nf, LANES), jnp.float32)] * 2,
        compiler_params=params(),
        cost_estimate=cost(20 * own.size, own, own),
        name="join",
    )(relax, side, speed, upwind, own, top, bottom, recv, *before)


def last_speed(fields_total, speed, solid, halo, stress, other, flow):
    return pl.pallas_call(
        functools.partial(last_kernel, fields_total),
        out_shape=shaped(speed.shape),
        in_specs=[vmem()] * 6,
        out_specs=vmem(),
        name="last_speed",
    )(speed, solid, halo, stress, other, flow)


def swapped(value, axis, bit):
    count = lax.axis_size(axis)
    return lax.ppermute(value, axis, [(i, i ^ bit) for i in range(count)])


def field_sum(value):
    bit = 1
    while 2 * bit < lax.axis_size("field"):
        value = value + swapped(value, "field", bit)
        bit *= 2
    return value, swapped(value, "field", bit)


def flow_sums(sums, recv1, recv2):
    value = sums + recv1[recv1.shape[0] - 1 :].astype(jnp.float32)
    value = value + swapped(value, "slab", 2)
    value = value + swapped(value, "slab", 4)
    value, recv2 = lax.optimization_barrier((value, recv2))
    slabs, parts = lax.axis_size("slab"), lax.axis_size("field")
    assert slabs == 8 * parts
    pairs = [(((s + 8 * f) % slabs) * parts + f, s * parts + f) for s in range(slabs) for f in range(parts)]
    return lax.ppermute(value, ("slab", "field"), pairs), recv2


def per_device(conform, velocity, solid_mask, upwind, relax_time, wiener):
    slabs = lax.axis_size("slab")
    fields_total = conform.shape[1] * lax.axis_size("field")
    odd = (lax.axis_index("slab") % 2).astype(jnp.int32).reshape(1)
    near_pairs = [(i, i ^ 1) for i in range(slabs)]
    far_pairs = [(i, (i + 1) % slabs if i % 2 else (i - 1) % slabs) for i in range(slabs)]
    fields, speed, extra = conform, velocity, ()
    for step in range(STEPS):
        top, bottom, send1, send2, sums, speed = edge_steps(
            step, fields_total, relax_time, odd, speed, solid_mask, upwind, fields, wiener, extra
        )
        recv1 = lax.ppermute(send1, "slab", near_pairs)
        recv2 = lax.ppermute(send2, "slab", far_pairs)
        if step == 0:
            flow = lax.all_gather(sums, "slab", axis=0, tiled=True)
            recv1, flow = lax.optimization_barrier((recv1, flow))
        else:
            flow, recv2 = flow_sums(sums, recv1, recv2)
        own = own_steps(step, relax_time, speed, upwind, fields, wiener)
        fields, stress, halo = join(relax_time, odd, speed, upwind, own, top, bottom, recv1)
        fields, stress, halo = join(relax_time, 1 - odd, speed, upwind, fields, top, bottom, recv2, (stress, halo))
        if step > 0:
            stress = lax.dynamic_update_slice(stress, flow[None], (0, ROWS, 0))
        stress, other = field_sum(stress)
        if step > 0:
            flow = stress[0, ROWS : ROWS + 1] + other[0, ROWS : ROWS + 1]
        extra = (halo, stress, other, flow)
    speed = last_speed(fields_total, speed, solid_mask, *extra)
    return (fields, speed)


def solution(mesh):
    placed = (
        P(None, "field", "slab", None),
        P(None, "slab", None),
        P("slab", None),
        P(None, "slab", None),
        P("field"),
        P(None, None, "field", "slab", None),
    )
    return jax.shard_map(
        per_device,
        mesh=mesh,
        in_specs=placed,
        out_specs=(P(None, "field", "slab", None), P(None, "slab", None)),
        check_vma=False,
    )
```

```python
import functools
import jax
import jax.numpy as jnp
from jax import lax
from jax.experimental import pallas as pl
from jax.experimental.pallas import tpu as pltpu
from jax.sharding import PartitionSpec as P

STEPS = 2
SUBS = 3
ROWS = 16
LANES = 128

sub_step = 0.1
macro_step = 0.3
viscosity = 0.5
modulus = 4.0
target_flow = 0.8

TRACKS = 3 * SUBS + 2
SENT = 3 * SUBS + 3 + 4
KEPT = 0.85
EXTRA = 16
TOP_ROW = ROWS + 3
BOTTOM_ROW = ROWS + 4
UNROLL = 4
VMEM_LIMIT = 32 * 1024 * 1024


def left(v):
    return pltpu.roll(v, 1, 1)


def right(v):
    return pltpu.roll(v, LANES - 1, 1)


def above(v):
    return pltpu.roll(v, 1, 0)


def below(v):
    return pltpu.roll(v, v.shape[0] - 1, 0)


def row_index(rows):
    return lax.broadcasted_iota(jnp.int32, (rows, LANES), 0)


def neighbour_weights(speed, flag):
    step = sub_step * speed
    zero = jnp.zeros_like(step)
    return jnp.where(flag == 1, step, zero), jnp.where(flag == 1, zero, -step)


def split(v):
    first = v.astype(jnp.bfloat16).astype(jnp.float32)
    rest = v - first
    second = rest.astype(jnp.bfloat16).astype(jnp.float32)
    third = (rest - second).astype(jnp.bfloat16).astype(jnp.float32)
    return first, second, third


def total(flow, which):
    return flow[:, which : which + 1] + flow[:, which + 2 : which + 3] + flow[:, which + 4 : which + 5]


def updated_speed(fields_total, speed, halo_ref, stress_refs, fluid):
    row = row_index(ROWS)
    scale = modulus / fields_total

    def stress(c, rows):
        return scale * (stress_refs[0][c, rows, :] + stress_refs[1][c, rows, :]) - (modulus if c != 1 else 0.0)

    main = [stress(c, slice(0, ROWS)) for c in range(3)]
    before = [stress(c, slice(TOP_ROW, TOP_ROW + 1)) for c in range(3)]
    after = [stress(c, slice(BOTTOM_ROW, BOTTOM_ROW + 1)) for c in range(3)]
    flow = sum(ref[0, ROWS : ROWS + 1, :] for ref in stress_refs)
    mean_flow = total(flow, 0) / total(flow, 1)

    def up(v, edge):
        return jnp.where(row == 0, edge, above(v))

    def down(v, edge):
        return jnp.where(row == ROWS - 1, edge, below(v))

    new = []
    for c in range(2):
        v = speed[c]
        laplace = up(v, halo_ref[c : c + 1, :]) + down(v, halo_ref[2 + c : 3 + c, :]) + left(v) + right(v) - 4.0 * v
        along_x = down(main[c], after[c]) - up(main[c], before[c])
        along_y = right(main[c + 1]) - left(main[c + 1])
        divergence = along_x * 0.5 + along_y * 0.5
        v = v + macro_step * (divergence + viscosity * laplace)
        if c == 0:
            v = v + (target_flow - mean_flow)
        new.append(fluid * v)
    return new


def relaxation(relax_ref, f):
    relax = jnp.full((8, LANES), relax_ref[f], jnp.float32)
    return sub_step * (0.5 / relax), jnp.sqrt(sub_step / relax)


def doubled(v):
    return jnp.concatenate([v, v], axis=0)


def slab_weights(sx, sy, flag_x, flag_y):
    row = row_index(ROWS)
    zero = jnp.zeros((ROWS, LANES), jnp.float32)

    def grad_x(v):
        return (jnp.where(row == ROWS - 1, zero, below(v)) - jnp.where(row == 0, zero, above(v))) * 0.5

    def grad_y(v):
        return (right(v) - left(v)) * 0.5

    gxx, gxy = sub_step * grad_x(sx), sub_step * grad_x(sy)
    gyx, gyy = sub_step * grad_y(sx), sub_step * grad_y(sy)
    wa, wb = neighbour_weights(sx, flag_x)
    wl, wr = neighbour_weights(sy, flag_y)
    centre = 1.0 - wa - wb - wl - wr
    wa = jnp.where(row == 0, zero, wa)
    wb = jnp.where(row == ROWS - 1, zero, wb)
    return centre, wa, wb, wl, wr, gxx, gxy, gyx, gyy


def substep(q, diagonal, weights, extra):
    _, wa, wb, wl, wr, _, gxy, gyx, _ = weights
    new = []
    for c in range(3):
        v = q[c]
        acc = diagonal[c] * v + extra[c]
        acc = acc + (wl * left(v) + wr * right(v))
        acc = acc + (wa * above(v) + wb * below(v))
        if c == 0:
            acc = acc + gyx * q[1]
        elif c == 1:
            acc = acc + gxy * q[0]
        new.append(acc)
    return new


def edge_kernel(nf, fields_total, first, *refs):
    refs = list(refs)

    def take(count):
        taken = refs[:count]
        del refs[:count]
        return taken

    relax_ref, odd_ref, speed_ref, solid_ref, upwind_ref, fields_ref, wiener_ref = take(7)
    if not first:
        halo_ref, stress_ref, other_ref = take(3)
    top_ref, bottom_ref, send1_ref, send2_ref, sums_ref = take(5)
    if not first:
        (new_speed_ref,) = take(1)
    top_extra, bottom_extra = refs

    fluid = (1 - solid_ref[...]).astype(jnp.float32)
    sx, sy = speed_ref[0], speed_ref[1]
    if not first:
        sx, sy = updated_speed(fields_total, (sx, sy), halo_ref, (stress_ref, other_ref), fluid)
        new_speed_ref[0] = sx
        new_speed_ref[1] = sy
    flow = jnp.sum(jnp.sum(fluid * sx, axis=0, keepdims=True), axis=1, keepdims=True)
    cells = jnp.sum(jnp.sum(fluid, axis=0, keepdims=True), axis=1, keepdims=True)
    lane = lax.broadcasted_iota(jnp.int32, (1, LANES), 1)
    sums = jnp.where(lane == 0, flow, jnp.where(lane == 1, cells, 0.0))
    sums_ref[...] = sums

    row = row_index(8)
    flag_x, flag_y = upwind_ref[0], upwind_ref[1]

    def packed(v):
        return jnp.where(row < 4, v[0:8], v[8:16])

    weights = [packed(w) for w in slab_weights(sx, sy, flag_x, flag_y)]
    centre, gxx, gyy = weights[0], weights[5], weights[8]

    def body(f):
        delta, spread = relaxation(relax_ref, f)
        base = centre - delta
        diagonal = (base + gxx, base + gyy, base)
        q = [packed(fields_ref[c, f]) for c in range(3)]
        for k in range(SUBS + 1):
            for c in range(3 if k < SUBS else 2):
                top_ref[3 * k + c, pl.ds(f, 1), :] = q[c][0:1, :]
                bottom_ref[3 * k + c, pl.ds(f, 1), :] = q[c][7:8, :]
            if k < SUBS:
                kicks = [spread * packed(wiener_ref[k, c, f].astype(jnp.float32)) for c in range(3)]
                q = substep(q, diagonal, weights, kicks)

    def some(j, carry):
        for u in range(UNROLL):
            body(j * UNROLL + u)
        return carry

    lax.fori_loop(0, nf // UNROLL, some, 0)

    first_term, second_term, third_term = split(jnp.broadcast_to(sums, (8, LANES)))
    packed_sums = (first_term + pltpu.roll(second_term, 2, 1) + pltpu.roll(third_term, 4, 1))[0:1]
    terms = (split(sx), split(sy))
    flags = (flag_x.astype(jnp.float32), flag_y.astype(jnp.float32))
    for extra, near, far in ((top_extra, 0, 1), (bottom_extra, ROWS - 1, ROWS - 2)):
        for c in range(2):
            for i in range(3):
                extra[3 * c + i : 3 * c + i + 1, :] = terms[c][i][near : near + 1, :]
                extra[6 + 3 * c + i : 7 + 3 * c + i, :] = terms[c][i][far : far + 1, :]
        extra[12:13, :] = flags[0][near : near + 1, :]
        extra[13:14, :] = flags[1][near : near + 1, :]
        extra[14:15, :] = flags[0][far : far + 1, :]
        extra[15:16, :] = packed_sums

    odd = jnp.full((nf, LANES), odd_ref[0], jnp.int32) == 1
    for send_ref, one_ref, two_ref in ((send1_ref, top_ref, bottom_ref), (send2_ref, bottom_ref, top_ref)):

        def put(t, v):
            rounded = v.astype(jnp.bfloat16)
            send_ref[nf * t : nf * t + nf, :] = rounded
            return v - rounded.astype(jnp.float32)

        for c in range(3):
            error = jnp.zeros((nf, LANES), jnp.float32)
            for k in range(SUBS):
                error = put(3 * k + c, jnp.where(odd, one_ref[3 * k + c], two_ref[3 * k + c]) + KEPT * error)
            put(3 * SUBS + c, error)
            if c < 2:
                error = put(3 * SUBS + 3 + c, jnp.where(odd, one_ref[3 * SUBS + c], two_ref[3 * SUBS + c]))
                put(3 * SUBS + 5 + c, error)
    odd = jnp.full((EXTRA, LANES), odd_ref[0], jnp.int32) == 1
    top, bottom = top_extra[...], bottom_extra[...]
    tail = nf * SENT
    send1_ref[tail : tail + EXTRA, :] = jnp.where(odd, top, bottom).astype(jnp.bfloat16)
    send2_ref[tail : tail + EXTRA, :] = jnp.where(odd, bottom, top).astype(jnp.bfloat16)


def own_kernel(nf, relax_ref, speed_ref, upwind_ref, fields_ref, wiener_ref, out_ref):
    weights = slab_weights(speed_ref[0], speed_ref[1], upwind_ref[0], upwind_ref[1])
    centre, gxx, gyy = weights[0], weights[5], weights[8]

    def body(f):
        delta, spread = [doubled(v) for v in relaxation(relax_ref, f)]
        base = centre - delta
        diagonal = (base + gxx, base + gyy, base)
        q = [fields_ref[c, f] for c in range(3)]
        for k in range(SUBS):
            kicks = [spread * wiener_ref[k, c, f].astype(jnp.float32) for c in range(3)]
            q = substep(q, diagonal, weights, kicks)
        for c in range(3):
            out_ref[c, f] = q[c]

    def some(j, carry):
        for u in range(UNROLL):
            body(j * UNROLL + u)
        return carry

    lax.fori_loop(0, nf // UNROLL, some, 0)


def join_kernel(nf, first, *refs):
    refs = list(refs)
    relax_ref, side_ref, speed_ref, upwind_ref, own_ref, top_ref, bottom_ref, recv_ref = refs[:8]
    refs = refs[8:]
    if not first:
        stress_in, halo_in = refs[:2]
        refs = refs[2:]
    out_ref, stress_ref, halo_ref, upper_ref, lower_ref = refs
    side = side_ref[0]
    top = jnp.full((nf, LANES), side, jnp.int32) == 1
    last = 3 * (SUBS - 1)
    for t in range(TRACKS):
        if t < last:
            places = (t,)
        elif t < 3 * SUBS:
            places = (t, t + 3)
        else:
            places = (t + 3, t + 5)
        terms = [recv_ref[nf * p : nf * p + nf, :].astype(jnp.float32) for p in places]
        got = sum(terms[1:], terms[0])
        upper_ref[t] = jnp.where(top, got, bottom_ref[t])
        lower_ref[t] = jnp.where(top, top_ref[t], got)
    tail = nf * SENT
    extra = recv_ref[tail : tail + EXTRA, :].astype(jnp.float32)

    row = row_index(8)
    top = jnp.full((8, LANES), side, jnp.int32) == 1
    zero = jnp.zeros((8, LANES), jnp.float32)
    own_rows = (top & (row >= 4)) | (~top & (row < 4))
    near_row = (top & (row == 3)) | (~top & (row == 4))
    far_row = (top & (row == 2)) | (~top & (row == 5))

    def strip(values, near, far):
        own = pltpu.roll(jnp.where(top, values[0:8], values[8:16]), 4, 0)
        return jnp.where(own_rows, own, jnp.where(near_row, near, jnp.where(far_row, far, zero)))

    def joined(i):
        return extra[i : i + 1, :] + extra[i + 1 : i + 2, :] + extra[i + 2 : i + 3, :]

    near_x, near_y = joined(0), joined(3)
    halo = jnp.where(row % 2 == 0, near_x, near_y)
    mine = (top & (row < 2)) | (~top & (row >= 2) & (row < 4))
    halo = jnp.where(mine, halo, zero)
    halo_ref[...] = halo if first else halo + halo_in[...]
    sx = strip(speed_ref[0], near_x, joined(6))
    sy = strip(speed_ref[1], near_y, joined(9))
    flag_x = strip(upwind_ref[0].astype(jnp.float32), extra[12:13, :], extra[14:15, :])
    flag_y = strip(upwind_ref[1].astype(jnp.float32), extra[13:14, :], zero)

    upper = row == 3
    lower = row == 4
    half = 0.5 * sub_step
    gxx = half * (below(sx) - above(sx))
    gxy = half * (below(sy) - above(sy))
    gyx = half * (right(sx) - left(sx))
    gyy = half * (right(sy) - left(sy))
    wa, wb = neighbour_weights(sx, flag_x)
    wl, wr = neighbour_weights(sy, flag_y)
    centre = 1.0 - wa - wb - wl - wr
    weights = (centre, wa, wb, wl, wr, gxx, gxy, gyx, gyy)
    from_upper = jnp.where(lower, wa, zero)
    from_lower = jnp.where(upper, wb, zero)
    upper_y = jnp.where(upper, half * below(sy), zero)
    lower_y = jnp.where(lower, -half * above(sy), zero)
    from_upper_x = from_upper + jnp.where(upper, half * below(sx), zero)
    from_lower_x = from_lower + jnp.where(lower, -half * above(sx), zero)
    start = pl.multiple_of((1 - side) * 8, 8)

    def body(f, sums):
        delta, _ = relaxation(relax_ref, f)
        base = centre - delta
        diagonal = (base + gxx, base + gyy, base)

        def spread_row(ref, t):
            return jnp.broadcast_to(ref[t, pl.ds(f, 1), :], (8, LANES))

        d = None
        for k in range(SUBS):
            hu = [spread_row(upper_ref, 3 * k + c) for c in range(3)]
            hl = [spread_row(lower_ref, 3 * k + c) for c in range(3)]
            new = [
                from_upper_x * hu[0] + from_lower_x * hl[0],
                from_upper * hu[1] + from_lower * hl[1] + (upper_y * hu[0] + lower_y * hl[0]),
                from_upper * hu[2] + from_lower * hl[2],
            ]
            d = new if d is None else substep(d, diagonal, weights, new)
        full = []
        edge = []
        for c in range(3):
            half_rows = own_ref[c, f, pl.ds(start, 8), :]
            v = half_rows + pltpu.roll(jnp.where(own_rows, d[c], zero), 4, 0)
            out_ref[c, f, pl.ds(start, 8), :] = v
            rest = pl.multiple_of(8 - start, 8)
            out_ref[c, f, pl.ds(rest, 8), :] = own_ref[c, f, pl.ds(rest, 8), :]
            if c < 2:
                t = 3 * SUBS + c
                full.append(v)
                edge.append(d[c] + jnp.where(upper, spread_row(upper_ref, t), spread_row(lower_ref, t)))
        pairs = ((0, 0), (0, 1), (1, 1))
        return tuple(s + full[i] * full[j] for s, (i, j) in zip(sums[:3], pairs)) + tuple(
            s + edge[i] * edge[j] for s, (i, j) in zip(sums[3:], pairs)
        )

    def some(j, sums):
        for u in range(UNROLL):
            sums = body(j * UNROLL + u, sums)
        return sums

    sums = lax.fori_loop(0, nf // UNROLL, some, (zero,) * 6)
    for c in range(3):
        edge = jnp.where(near_row, sums[3 + c], zero)
        if first:
            stress_ref[c, 0:ROWS, :] = jnp.zeros((ROWS, LANES), jnp.float32)
        else:
            stress_ref[c, 0:ROWS, :] = stress_in[c, 0:ROWS, :]
            edge = edge + stress_in[c, ROWS : ROWS + 8, :]
        stress_ref[c, pl.ds(start, 8), :] = sums[c]
        stress_ref[c, ROWS : ROWS + 8, :] = edge


def last_kernel(fields_total, speed_ref, solid_ref, halo_ref, stress_ref, other_ref, out_ref):
    fluid = (1 - solid_ref[...]).astype(jnp.float32)
    speed = (speed_ref[0], speed_ref[1])
    sx, sy = updated_speed(fields_total, speed, halo_ref, (stress_ref, other_ref), fluid)
    out_ref[0] = sx
    out_ref[1] = sy


def vmem():
    return pl.BlockSpec(memory_space=pltpu.VMEM)


def smem():
    return pl.BlockSpec(memory_space=pltpu.SMEM)


def shaped(shape, dtype=jnp.float32):
    return jax.ShapeDtypeStruct(shape, dtype)


def whole(shape):
    return pl.BlockSpec(shape, lambda i: (0,) * len(shape))


def step_block(step, shape):
    return pl.BlockSpec((SUBS,) + shape[1:], lambda i: (step,) + (0,) * (len(shape) - 1))


def cost(flops, *arrays):
    size = sum(v.size * v.dtype.itemsize for v in arrays)
    return pl.CostEstimate(flops=flops, bytes_accessed=size, transcendentals=0)


def params():
    return pltpu.CompilerParams(vmem_limit_bytes=VMEM_LIMIT)


def edge_steps(step, fields_total, relax, odd, speed, solid, upwind, fields, wiener, extra):
    nf = fields.shape[1]
    first = step == 0
    size = nf * SENT + EXTRA
    outs = [
        shaped((TRACKS, nf, LANES)),
        shaped((TRACKS, nf, LANES)),
        shaped((size, LANES), jnp.bfloat16),
        shaped((size, LANES), jnp.bfloat16),
        shaped((1, LANES)),
    ]
    if not first:
        outs.append(shaped(speed.shape))
    got = pl.pallas_call(
        functools.partial(edge_kernel, nf, fields_total, first),
        grid=(1,),
        out_shape=outs,
        in_specs=[smem(), smem()]
        + [whole(v.shape) for v in (speed, solid, upwind, fields)]
        + [step_block(step, wiener.shape)]
        + [whole(v.shape) for v in extra],
        out_specs=[whole(o.shape) for o in outs],
        scratch_shapes=[pltpu.VMEM((EXTRA, LANES), jnp.float32)] * 2,
        compiler_params=params(),
        name="edge_steps",
    )(relax, odd, speed, solid, upwind, fields, wiener, *extra)
    return list(got) + ([speed] if first else [])


def own_steps(step, relax, speed, upwind, fields, wiener):
    return pl.pallas_call(
        functools.partial(own_kernel, fields.shape[1]),
        grid=(1,),
        out_shape=shaped(fields.shape),
        in_specs=[smem()] + [whole(v.shape) for v in (speed, upwind, fields)] + [step_block(step, wiener.shape)],
        out_specs=whole(fields.shape),
        compiler_params=params(),
        cost_estimate=cost(60 * fields.size, fields, fields, fields),
        name="own_steps",
    )(relax, speed, upwind, fields, wiener)


def join(relax, side, speed, upwind, own, top, bottom, recv, before=()):
    nf = own.shape[1]
    return pl.pallas_call(
        functools.partial(join_kernel, nf, not before),
        out_shape=[shaped(own.shape), shaped((3, ROWS + 8, LANES)), shaped((8, LANES))],
        in_specs=[smem(), smem()] + [vmem()] * (6 + len(before)),
        out_specs=[vmem()] * 3,
        scratch_shapes=[pltpu.VMEM((TRACKS, nf, LANES), jnp.float32)] * 2,
        compiler_params=params(),
        cost_estimate=cost(20 * own.size, own, own),
        name="join",
    )(relax, side, speed, upwind, own, top, bottom, recv, *before)


def last_speed(fields_total, speed, solid, halo, stress, other):
    return pl.pallas_call(
        functools.partial(last_kernel, fields_total),
        out_shape=shaped(speed.shape),
        in_specs=[vmem()] * 5,
        out_specs=vmem(),
        compiler_params=params(),
        name="last_speed",
    )(speed, solid, halo, stress, other)


def swapped(value, axis, bit):
    count = lax.axis_size(axis)
    return lax.ppermute(value, axis, [(i, i ^ bit) for i in range(count)])


def field_sum(value):
    bit = 1
    while 2 * bit < lax.axis_size("field"):
        value = value + swapped(value, "field", bit)
        bit *= 2
    return value, swapped(value, "field", bit)


def flow_sums(sums, recv1, recv2):
    value = sums + recv1[recv1.shape[0] - 1 :].astype(jnp.float32)
    value = value + swapped(value, "slab", 4)
    value = value + swapped(value, "slab", 2)
    value, recv2 = lax.optimization_barrier((value, recv2))
    slabs, parts = lax.axis_size("slab"), lax.axis_size("field")
    assert slabs == 8 * parts
    pairs = [(((s + 8 * f) % slabs) * parts + f, s * parts + f) for s in range(slabs) for f in range(parts)]
    return lax.ppermute(value, ("slab", "field"), pairs), recv2


def per_device(conform, velocity, solid_mask, upwind, relax_time, wiener):
    slabs = lax.axis_size("slab")
    fields_total = conform.shape[1] * lax.axis_size("field")
    odd = (lax.axis_index("slab") % 2).astype(jnp.int32).reshape(1)
    near_pairs = [(i, i ^ 1) for i in range(slabs)]
    far_pairs = [(i, (i + 1) % slabs if i % 2 else (i - 1) % slabs) for i in range(slabs)]
    fields, speed, extra = conform, velocity, ()
    for step in range(STEPS):
        top, bottom, send1, send2, sums, speed = edge_steps(
            step, fields_total, relax_time, odd, speed, solid_mask, upwind, fields, wiener, extra
        )
        recv1 = lax.ppermute(send1, "slab", near_pairs)
        recv2 = lax.ppermute(send2, "slab", far_pairs)
        flow, recv2 = flow_sums(sums, recv1, recv2)
        own = own_steps(step, relax_time, speed, upwind, fields, wiener)
        fields, stress, halo = join(relax_time, odd, speed, upwind, own, top, bottom, recv1)
        fields, stress, halo = join(relax_time, 1 - odd, speed, upwind, fields, top, bottom, recv2, (stress, halo))
        stress = lax.dynamic_update_slice(stress, flow[None], (0, ROWS, 0))
        extra = (halo,) + field_sum(stress)
    speed = last_speed(fields_total, speed, solid_mask, *extra)
    return (fields, speed)


def solution(mesh):
    placed = (
        P(None, "field", "slab", None),
        P(None, "slab", None),
        P("slab", None),
        P(None, "slab", None),
        P("field"),
        P(None, None, "field", "slab", None),
    )
    return jax.shard_map(
        per_device,
        mesh=mesh,
        in_specs=placed,
        out_specs=(P(None, "field", "slab", None), P(None, "slab", None)),
        check_vma=False,
    )
```

```python
import functools
import jax
import jax.numpy as jnp
from jax import lax
from jax.experimental import pallas as pl
from jax.experimental.pallas import tpu as pltpu
from jax.sharding import PartitionSpec as P

STEPS = 2
SUBS = 3
ROWS = 16
LANES = 128

sub_step = 0.1
macro_step = 0.3
viscosity = 0.5
modulus = 4.0
target_flow = 0.8

TRACKS = 3 * SUBS + 2
SENT = 3 * SUBS + 3 + 4
KEPT = 0.85
EXTRA = 16
TOP_ROW = ROWS + 3
BOTTOM_ROW = ROWS + 4
UNROLL = 4
VMEM_LIMIT = 32 * 1024 * 1024


def left(v):
    return pltpu.roll(v, 1, 1)


def right(v):
    return pltpu.roll(v, LANES - 1, 1)


def above(v):
    return pltpu.roll(v, 1, 0)


def below(v):
    return pltpu.roll(v, v.shape[0] - 1, 0)


def row_index(rows):
    return lax.broadcasted_iota(jnp.int32, (rows, LANES), 0)


def neighbour_weights(speed, flag):
    step = sub_step * speed
    zero = jnp.zeros_like(step)
    return jnp.where(flag == 1, step, zero), jnp.where(flag == 1, zero, -step)


def split(v):
    first = v.astype(jnp.bfloat16).astype(jnp.float32)
    rest = v - first
    second = rest.astype(jnp.bfloat16).astype(jnp.float32)
    third = (rest - second).astype(jnp.bfloat16).astype(jnp.float32)
    return first, second, third


def total(flow, which):
    return flow[:, which : which + 1] + flow[:, which + 2 : which + 3] + flow[:, which + 4 : which + 5]


def pairwise(terms):
    while len(terms) > 1:
        terms = [terms[i] + terms[i + 1] for i in range(0, len(terms), 2)]
    return terms[0]


def updated_speed(fields_total, speed, halo_ref, stress_refs, fluid):
    row = row_index(ROWS)
    scale = modulus / fields_total

    def stress(c, rows):
        return scale * pairwise([ref[c, rows, :] for ref in stress_refs]) - (modulus if c != 1 else 0.0)

    main = [stress(c, slice(0, ROWS)) for c in range(3)]
    before = [stress(c, slice(TOP_ROW, TOP_ROW + 1)) for c in range(3)]
    after = [stress(c, slice(BOTTOM_ROW, BOTTOM_ROW + 1)) for c in range(3)]
    flow = pairwise([ref[0, ROWS : ROWS + 1, :] for ref in stress_refs])
    mean_flow = total(flow, 0) / total(flow, 1)

    def up(v, edge):
        return jnp.where(row == 0, edge, above(v))

    def down(v, edge):
        return jnp.where(row == ROWS - 1, edge, below(v))

    new = []
    for c in range(2):
        v = speed[c]
        laplace = up(v, halo_ref[c : c + 1, :]) + down(v, halo_ref[2 + c : 3 + c, :]) + left(v) + right(v) - 4.0 * v
        along_x = down(main[c], after[c]) - up(main[c], before[c])
        along_y = right(main[c + 1]) - left(main[c + 1])
        divergence = along_x * 0.5 + along_y * 0.5
        v = v + macro_step * (divergence + viscosity * laplace)
        if c == 0:
            v = v + (target_flow - mean_flow)
        new.append(fluid * v)
    return new


def relaxation(relax_ref, f):
    relax = jnp.full((8, LANES), relax_ref[f], jnp.float32)
    return sub_step * (0.5 / relax), jnp.sqrt(sub_step / relax)


def doubled(v):
    return jnp.concatenate([v, v], axis=0)


def slab_weights(sx, sy, flag_x, flag_y):
    row = row_index(ROWS)
    zero = jnp.zeros((ROWS, LANES), jnp.float32)

    def grad_x(v):
        return (jnp.where(row == ROWS - 1, zero, below(v)) - jnp.where(row == 0, zero, above(v))) * 0.5

    def grad_y(v):
        return (right(v) - left(v)) * 0.5

    gxx, gxy = sub_step * grad_x(sx), sub_step * grad_x(sy)
    gyx, gyy = sub_step * grad_y(sx), sub_step * grad_y(sy)
    wa, wb = neighbour_weights(sx, flag_x)
    wl, wr = neighbour_weights(sy, flag_y)
    centre = 1.0 - wa - wb - wl - wr
    wa = jnp.where(row == 0, zero, wa)
    wb = jnp.where(row == ROWS - 1, zero, wb)
    return centre, wa, wb, wl, wr, gxx, gxy, gyx, gyy


def substep(q, diagonal, weights, extra):
    _, wa, wb, wl, wr, _, gxy, gyx, _ = weights
    new = []
    for c in range(3):
        v = q[c]
        acc = diagonal[c] * v + extra[c]
        acc = acc + (wl * left(v) + wr * right(v))
        acc = acc + (wa * above(v) + wb * below(v))
        if c == 0:
            acc = acc + gyx * q[1]
        elif c == 1:
            acc = acc + gxy * q[0]
        new.append(acc)
    return new


def edge_kernel(nf, fields_total, terms, *refs):
    refs = list(refs)

    def take(count):
        taken = refs[:count]
        del refs[:count]
        return taken

    relax_ref, odd_ref, speed_ref, solid_ref, upwind_ref, fields_ref, wiener_ref = take(7)
    first = terms == 0
    if not first:
        (halo_ref,) = take(1)
        stress_refs = take(terms)
    top_ref, bottom_ref, send1_ref, send2_ref, sums_ref = take(5)
    if not first:
        (new_speed_ref,) = take(1)
    top_extra, bottom_extra = refs

    fluid = (1 - solid_ref[...]).astype(jnp.float32)
    sx, sy = speed_ref[0], speed_ref[1]
    if not first:
        sx, sy = updated_speed(fields_total, (sx, sy), halo_ref, stress_refs, fluid)
        new_speed_ref[0] = sx
        new_speed_ref[1] = sy
    flow = jnp.sum(jnp.sum(fluid * sx, axis=0, keepdims=True), axis=1, keepdims=True)
    cells = jnp.sum(jnp.sum(fluid, axis=0, keepdims=True), axis=1, keepdims=True)
    lane = lax.broadcasted_iota(jnp.int32, (1, LANES), 1)
    sums = jnp.where(lane == 0, flow, jnp.where(lane == 1, cells, 0.0))
    sums_ref[...] = sums

    row = row_index(8)
    flag_x, flag_y = upwind_ref[0], upwind_ref[1]

    def packed(v):
        return jnp.where(row < 4, v[0:8], v[8:16])

    weights = [packed(w) for w in slab_weights(sx, sy, flag_x, flag_y)]
    centre, gxx, gyy = weights[0], weights[5], weights[8]

    def body(f):
        delta, spread = relaxation(relax_ref, f)
        base = centre - delta
        diagonal = (base + gxx, base + gyy, base)
        q = [packed(fields_ref[c, f]) for c in range(3)]
        for k in range(SUBS + 1):
            for c in range(3 if k < SUBS else 2):
                top_ref[3 * k + c, pl.ds(f, 1), :] = q[c][0:1, :]
                bottom_ref[3 * k + c, pl.ds(f, 1), :] = q[c][7:8, :]
            if k < SUBS:
                kicks = [spread * packed(wiener_ref[k, c, f].astype(jnp.float32)) for c in range(3)]
                q = substep(q, diagonal, weights, kicks)

    def some(j, carry):
        for u in range(UNROLL):
            body(j * UNROLL + u)
        return carry

    lax.fori_loop(0, nf // UNROLL, some, 0)

    first_term, second_term, third_term = split(jnp.broadcast_to(sums, (8, LANES)))
    packed_sums = (first_term + pltpu.roll(second_term, 2, 1) + pltpu.roll(third_term, 4, 1))[0:1]
    terms = (split(sx), split(sy))
    flags = (flag_x.astype(jnp.float32), flag_y.astype(jnp.float32))
    for extra, near, far in ((top_extra, 0, 1), (bottom_extra, ROWS - 1, ROWS - 2)):
        for c in range(2):
            for i in range(3):
                extra[3 * c + i : 3 * c + i + 1, :] = terms[c][i][near : near + 1, :]
                extra[6 + 3 * c + i : 7 + 3 * c + i, :] = terms[c][i][far : far + 1, :]
        extra[12:13, :] = flags[0][near : near + 1, :]
        extra[13:14, :] = flags[1][near : near + 1, :]
        extra[14:15, :] = flags[0][far : far + 1, :]
        extra[15:16, :] = packed_sums

    odd = jnp.full((nf, LANES), odd_ref[0], jnp.int32) == 1
    for send_ref, one_ref, two_ref in ((send1_ref, top_ref, bottom_ref), (send2_ref, bottom_ref, top_ref)):

        def put(t, v):
            rounded = v.astype(jnp.bfloat16)
            send_ref[nf * t : nf * t + nf, :] = rounded
            return v - rounded.astype(jnp.float32)

        for c in range(3):
            error = jnp.zeros((nf, LANES), jnp.float32)
            for k in range(SUBS):
                error = put(3 * k + c, jnp.where(odd, one_ref[3 * k + c], two_ref[3 * k + c]) + KEPT * error)
            put(3 * SUBS + c, error)
            if c < 2:
                error = put(3 * SUBS + 3 + c, jnp.where(odd, one_ref[3 * SUBS + c], two_ref[3 * SUBS + c]))
                put(3 * SUBS + 5 + c, error)
    odd = jnp.full((EXTRA, LANES), odd_ref[0], jnp.int32) == 1
    top, bottom = top_extra[...], bottom_extra[...]
    tail = nf * SENT
    send1_ref[tail : tail + EXTRA, :] = jnp.where(odd, top, bottom).astype(jnp.bfloat16)
    send2_ref[tail : tail + EXTRA, :] = jnp.where(odd, bottom, top).astype(jnp.bfloat16)


def own_kernel(nf, relax_ref, speed_ref, upwind_ref, fields_ref, wiener_ref, out_ref):
    weights = slab_weights(speed_ref[0], speed_ref[1], upwind_ref[0], upwind_ref[1])
    centre, gxx, gyy = weights[0], weights[5], weights[8]

    def body(f):
        delta, spread = [doubled(v) for v in relaxation(relax_ref, f)]
        base = centre - delta
        diagonal = (base + gxx, base + gyy, base)
        q = [fields_ref[c, f] for c in range(3)]
        for k in range(SUBS):
            kicks = [spread * wiener_ref[k, c, f].astype(jnp.float32) for c in range(3)]
            q = substep(q, diagonal, weights, kicks)
        for c in range(3):
            out_ref[c, f] = q[c]

    def some(j, carry):
        for u in range(UNROLL):
            body(j * UNROLL + u)
        return carry

    lax.fori_loop(0, nf // UNROLL, some, 0)


def join_kernel(nf, first, *refs):
    refs = list(refs)
    relax_ref, side_ref, speed_ref, upwind_ref, own_ref, top_ref, bottom_ref, recv_ref = refs[:8]
    refs = refs[8:]
    if not first:
        stress_in, halo_in = refs[:2]
        refs = refs[2:]
    out_ref, stress_ref, halo_ref, upper_ref, lower_ref = refs
    side = side_ref[0]
    top = jnp.full((nf, LANES), side, jnp.int32) == 1
    last = 3 * (SUBS - 1)
    for t in range(TRACKS):
        if t < last:
            places = (t,)
        elif t < 3 * SUBS:
            places = (t, t + 3)
        else:
            places = (t + 3, t + 5)
        terms = [recv_ref[nf * p : nf * p + nf, :].astype(jnp.float32) for p in places]
        got = sum(terms[1:], terms[0])
        upper_ref[t] = jnp.where(top, got, bottom_ref[t])
        lower_ref[t] = jnp.where(top, top_ref[t], got)
    tail = nf * SENT
    extra = recv_ref[tail : tail + EXTRA, :].astype(jnp.float32)

    row = row_index(8)
    top = jnp.full((8, LANES), side, jnp.int32) == 1
    zero = jnp.zeros((8, LANES), jnp.float32)
    own_rows = (top & (row >= 4)) | (~top & (row < 4))
    near_row = (top & (row == 3)) | (~top & (row == 4))
    far_row = (top & (row == 2)) | (~top & (row == 5))

    def strip(values, near, far):
        own = pltpu.roll(jnp.where(top, values[0:8], values[8:16]), 4, 0)
        return jnp.where(own_rows, own, jnp.where(near_row, near, jnp.where(far_row, far, zero)))

    def joined(i):
        return extra[i : i + 1, :] + extra[i + 1 : i + 2, :] + extra[i + 2 : i + 3, :]

    near_x, near_y = joined(0), joined(3)
    halo = jnp.where(row % 2 == 0, near_x, near_y)
    mine = (top & (row < 2)) | (~top & (row >= 2) & (row < 4))
    halo = jnp.where(mine, halo, zero)
    halo_ref[...] = halo if first else halo + halo_in[...]
    sx = strip(speed_ref[0], near_x, joined(6))
    sy = strip(speed_ref[1], near_y, joined(9))
    flag_x = strip(upwind_ref[0].astype(jnp.float32), extra[12:13, :], extra[14:15, :])
    flag_y = strip(upwind_ref[1].astype(jnp.float32), extra[13:14, :], zero)

    upper = row == 3
    lower = row == 4
    half = 0.5 * sub_step
    gxx = half * (below(sx) - above(sx))
    gxy = half * (below(sy) - above(sy))
    gyx = half * (right(sx) - left(sx))
    gyy = half * (right(sy) - left(sy))
    wa, wb = neighbour_weights(sx, flag_x)
    wl, wr = neighbour_weights(sy, flag_y)
    centre = 1.0 - wa - wb - wl - wr
    weights = (centre, wa, wb, wl, wr, gxx, gxy, gyx, gyy)
    from_upper = jnp.where(lower, wa, zero)
    from_lower = jnp.where(upper, wb, zero)
    upper_y = jnp.where(upper, half * below(sy), zero)
    lower_y = jnp.where(lower, -half * above(sy), zero)
    from_upper_x = from_upper + jnp.where(upper, half * below(sx), zero)
    from_lower_x = from_lower + jnp.where(lower, -half * above(sx), zero)
    start = pl.multiple_of((1 - side) * 8, 8)

    def body(f, sums):
        delta, _ = relaxation(relax_ref, f)
        base = centre - delta
        diagonal = (base + gxx, base + gyy, base)

        def spread_row(ref, t):
            return jnp.broadcast_to(ref[t, pl.ds(f, 1), :], (8, LANES))

        d = None
        for k in range(SUBS):
            hu = [spread_row(upper_ref, 3 * k + c) for c in range(3)]
            hl = [spread_row(lower_ref, 3 * k + c) for c in range(3)]
            new = [
                from_upper_x * hu[0] + from_lower_x * hl[0],
                from_upper * hu[1] + from_lower * hl[1] + (upper_y * hu[0] + lower_y * hl[0]),
                from_upper * hu[2] + from_lower * hl[2],
            ]
            d = new if d is None else substep(d, diagonal, weights, new)
        full = []
        edge = []
        for c in range(3):
            half_rows = own_ref[c, f, pl.ds(start, 8), :]
            v = half_rows + pltpu.roll(jnp.where(own_rows, d[c], zero), 4, 0)
            out_ref[c, f, pl.ds(start, 8), :] = v
            rest = pl.multiple_of(8 - start, 8)
            out_ref[c, f, pl.ds(rest, 8), :] = own_ref[c, f, pl.ds(rest, 8), :]
            if c < 2:
                t = 3 * SUBS + c
                full.append(v)
                edge.append(d[c] + jnp.where(upper, spread_row(upper_ref, t), spread_row(lower_ref, t)))
        pairs = ((0, 0), (0, 1), (1, 1))
        return tuple(s + full[i] * full[j] for s, (i, j) in zip(sums[:3], pairs)) + tuple(
            s + edge[i] * edge[j] for s, (i, j) in zip(sums[3:], pairs)
        )

    def some(j, sums):
        for u in range(UNROLL):
            sums = body(j * UNROLL + u, sums)
        return sums

    sums = lax.fori_loop(0, nf // UNROLL, some, (zero,) * 6)
    for c in range(3):
        edge = jnp.where(near_row, sums[3 + c], zero)
        if first:
            stress_ref[c, 0:ROWS, :] = jnp.zeros((ROWS, LANES), jnp.float32)
        else:
            stress_ref[c, 0:ROWS, :] = stress_in[c, 0:ROWS, :]
            edge = edge + stress_in[c, ROWS : ROWS + 8, :]
        stress_ref[c, pl.ds(start, 8), :] = sums[c]
        stress_ref[c, ROWS : ROWS + 8, :] = edge


def last_kernel(fields_total, speed_ref, solid_ref, halo_ref, *refs):
    stress_refs, out_ref = refs[:-1], refs[-1]
    fluid = (1 - solid_ref[...]).astype(jnp.float32)
    speed = (speed_ref[0], speed_ref[1])
    sx, sy = updated_speed(fields_total, speed, halo_ref, stress_refs, fluid)
    out_ref[0] = sx
    out_ref[1] = sy


def vmem():
    return pl.BlockSpec(memory_space=pltpu.VMEM)


def smem():
    return pl.BlockSpec(memory_space=pltpu.SMEM)


def shaped(shape, dtype=jnp.float32):
    return jax.ShapeDtypeStruct(shape, dtype)


def whole(shape):
    return pl.BlockSpec(shape, lambda i: (0,) * len(shape))


def step_block(step, shape):
    return pl.BlockSpec((SUBS,) + shape[1:], lambda i: (step,) + (0,) * (len(shape) - 1))


def cost(flops, *arrays):
    size = sum(v.size * v.dtype.itemsize for v in arrays)
    return pl.CostEstimate(flops=flops, bytes_accessed=size, transcendentals=0)


def params():
    return pltpu.CompilerParams(vmem_limit_bytes=VMEM_LIMIT)


def edge_steps(step, fields_total, relax, odd, speed, solid, upwind, fields, wiener, extra):
    nf = fields.shape[1]
    first = step == 0
    size = nf * SENT + EXTRA
    outs = [
        shaped((TRACKS, nf, LANES)),
        shaped((TRACKS, nf, LANES)),
        shaped((size, LANES), jnp.bfloat16),
        shaped((size, LANES), jnp.bfloat16),
        shaped((1, LANES)),
    ]
    if not first:
        outs.append(shaped(speed.shape))
    got = pl.pallas_call(
        functools.partial(edge_kernel, nf, fields_total, max(0, len(extra) - 1)),
        grid=(1,),
        out_shape=outs,
        in_specs=[smem(), smem()]
        + [whole(v.shape) for v in (speed, solid, upwind, fields)]
        + [step_block(step, wiener.shape)]
        + [whole(v.shape) for v in extra],
        out_specs=[whole(o.shape) for o in outs],
        scratch_shapes=[pltpu.VMEM((EXTRA, LANES), jnp.float32)] * 2,
        compiler_params=params(),
        name="edge_steps",
    )(relax, odd, speed, solid, upwind, fields, wiener, *extra)
    return list(got) + ([speed] if first else [])


def own_steps(step, relax, speed, upwind, fields, wiener):
    return pl.pallas_call(
        functools.partial(own_kernel, fields.shape[1]),
        grid=(1,),
        out_shape=shaped(fields.shape),
        in_specs=[smem()] + [whole(v.shape) for v in (speed, upwind, fields)] + [step_block(step, wiener.shape)],
        out_specs=whole(fields.shape),
        compiler_params=params(),
        cost_estimate=cost(60 * fields.size, fields, fields, fields),
        name="own_steps",
    )(relax, speed, upwind, fields, wiener)


def join(relax, side, speed, upwind, own, top, bottom, recv, before=()):
    nf = own.shape[1]
    return pl.pallas_call(
        functools.partial(join_kernel, nf, not before),
        out_shape=[shaped(own.shape), shaped((3, ROWS + 8, LANES)), shaped((8, LANES))],
        in_specs=[smem(), smem()] + [vmem()] * (6 + len(before)),
        out_specs=[vmem()] * 3,
        scratch_shapes=[pltpu.VMEM((TRACKS, nf, LANES), jnp.float32)] * 2,
        compiler_params=params(),
        cost_estimate=cost(20 * own.size, own, own),
        name="join",
    )(relax, side, speed, upwind, own, top, bottom, recv, *before)


def last_speed(fields_total, speed, solid, halo, *stresses):
    return pl.pallas_call(
        functools.partial(last_kernel, fields_total),
        out_shape=shaped(speed.shape),
        in_specs=[vmem()] * (3 + len(stresses)),
        out_specs=vmem(),
        compiler_params=params(),
        name="last_speed",
    )(speed, solid, halo, *stresses)


def swapped(value, axis, bit):
    count = lax.axis_size(axis)
    return lax.ppermute(value, axis, [(i, i ^ bit) for i in range(count)])


def field_sum(value):
    value = value + swapped(value, "field", 1)
    return (value,) + tuple(swapped(value, "field", bits) for bits in range(2, lax.axis_size("field"), 2))


def flow_sums(sums, recv1, recv2):
    value = sums + recv1[recv1.shape[0] - 1 :].astype(jnp.float32)
    value = value + swapped(value, "slab", 4)
    value = value + swapped(value, "slab", 2)
    value, recv2 = lax.optimization_barrier((value, recv2))
    slabs, parts = lax.axis_size("slab"), lax.axis_size("field")
    assert slabs == 8 * parts
    pairs = [(((s + 8 * f) % slabs) * parts + f, s * parts + f) for s in range(slabs) for f in range(parts)]
    return lax.ppermute(value, ("slab", "field"), pairs), recv2


def per_device(conform, velocity, solid_mask, upwind, relax_time, wiener):
    slabs = lax.axis_size("slab")
    fields_total = conform.shape[1] * lax.axis_size("field")
    odd = (lax.axis_index("slab") % 2).astype(jnp.int32).reshape(1)
    near_pairs = [(i, i ^ 1) for i in range(slabs)]
    far_pairs = [(i, (i + 1) % slabs if i % 2 else (i - 1) % slabs) for i in range(slabs)]
    fields, speed, extra = conform, velocity, ()
    for step in range(STEPS):
        top, bottom, send1, send2, sums, speed = edge_steps(
            step, fields_total, relax_time, odd, speed, solid_mask, upwind, fields, wiener, extra
        )
        recv1 = lax.ppermute(send1, "slab", near_pairs)
        recv2 = lax.ppermute(send2, "slab", far_pairs)
        flow, recv2 = flow_sums(sums, recv1, recv2)
        own = own_steps(step, relax_time, speed, upwind, fields, wiener)
        fields, stress, halo = join(relax_time, odd, speed, upwind, own, top, bottom, recv1)
        fields, stress, halo = join(relax_time, 1 - odd, speed, upwind, fields, top, bottom, recv2, (stress, halo))
        stress = lax.dynamic_update_slice(stress, flow[None], (0, ROWS, 0))
        extra = (halo,) + field_sum(stress)
    speed = last_speed(fields_total, speed, solid_mask, *extra)
    return (fields, speed)


def solution(mesh):
    placed = (
        P(None, "field", "slab", None),
        P(None, "slab", None),
        P("slab", None),
        P(None, "slab", None),
        P("field"),
        P(None, None, "field", "slab", None),
    )
    return jax.shard_map(
        per_device,
        mesh=mesh,
        in_specs=placed,
        out_specs=(P(None, "field", "slab", None), P(None, "slab", None)),
        check_vma=False,
    )
```
